256 devices in a mesh: expert: 64 (over z, y, core), replica: 4 (over x).
Axes of the slice: x: 4, y: 4, z: 8, core: 2. Of those that a mesh axis runs over, the one named last changes fastest.
Arguments:
- inputs: bfloat16 [32768, 2048], P(('expert', 'replica')), may hold values from -16 to 16
- cotangent: bfloat16 [32768, 2048], P(('expert', 'replica')), may hold values from -4 to 4
- routes: int32 [32768, 8], P(('expert', 'replica')), may hold values from 0 to 63, as said below
- router: bfloat16 [2048, 64], replicated, may hold values from -2 to 2
- w_gate: bfloat16 [64, 2048, 384], P('expert'), may hold values from -0.125 to 0.125
- w_up: bfloat16 [64, 2048, 384], P('expert'), may hold values from -0.125 to 0.125
- w_down: bfloat16 [64, 384, 2048], P('expert'), may hold values from -0.3125 to 0.3125
Outputs:
- grad_inputs: bfloat16 [32768, 2048], P(('expert', 'replica'))
- grad_router: float32 [2048, 64], replicated
The draws below stay inside these ranges and needn't reach their ends.
Inputs may be any that keep to these rules, and one draw needn't show every extreme that they name: `routes`: among the tokens of one device, the same 2 experts as on every device of its replica group (the devices with equal replica index) each fill exactly 56 of the 1024 choices, and every other expert fills at most 16.
All inputs are finite; a program needn't handle non-finite values.
Results may differ from the reference program's by a relative error of at most 0.0075.
Values may be sent and summed in bfloat16 or wider, within the bound.
No kernel may reach another device: no remote copies, remote signals or barrier semaphores. Data moves between devices by JAX's collectives and lax.ppermute only.
A program may use at most 128 MiB of HBM per device.

```python
import math
import jax
import jax.numpy as jnp
from jax import lax

D = 2048
FF = 384
TOK_DEV = 128
TOPK = 8
HELPERS = 5
EXPERTS = 64
TOKENS = 32768
CAP_OWN = 16
CAP_GST = 8
HOT = 2
N_REPLICA = 4


def input_rows(key):
    key = jax.random.fold_in(key, 11)
    first, second = jax.random.split(key)
    values = jnp.clip(jax.random.normal(first, (TOKENS, D), jnp.float32), -4.0, 4.0)
    scales = jnp.exp(jax.random.uniform(second, (TOKENS, 1), jnp.float32, 0.0, 1e-09))
    return values * scales


def route_table(key):
    key = jax.random.fold_in(key, 7)
    hot_load = CAP_OWN + HELPERS * CAP_GST
    need = TOK_DEV * TOPK - HOT * hot_load
    pool = EXPERTS * CAP_OWN
    pool_label = jnp.arange(pool, dtype=jnp.int32) // CAP_OWN

    def one_block(index):
        group_key = jax.random.fold_in(key, index % N_REPLICA + 1000003)
        hot_ids = jax.random.permutation(group_key, EXPERTS)[:HOT].astype(jnp.int32)
        hot_mark = jnp.zeros((EXPERTS,), jnp.int32).at[hot_ids].set(1)
        own_key = jax.random.fold_in(key, index)
        first, second, third = jax.random.split(own_key, 3)
        scores = jax.random.permutation(first, pool).astype(jnp.int32) - pool * hot_mark[pool_label]
        picked = lax.top_k(scores, need)[1]
        cold_labels = pool_label[picked]
        hot_labels = jnp.repeat(jnp.sort(hot_ids), hot_load)
        labels = jnp.sort(jnp.concatenate([hot_labels, cold_labels]))
        table = labels.reshape(TOPK, TOK_DEV).T
        table = table[jax.random.permutation(second, TOK_DEV)]
        row_keys = jax.random.split(third, TOK_DEV)
        col_perm = jax.vmap(lambda k: jax.random.permutation(k, TOPK))(row_keys)
        return jnp.take_along_axis(table, col_perm, axis=1).astype(jnp.int32)
    blocks = lax.map(one_block, jnp.arange(TOKENS // TOK_DEV, dtype=jnp.int32))
    return blocks.reshape(TOKENS, TOPK)


def draw_routes(key, part):
    table = route_table(key)
    return table


def draw_inputs(key, part):
    shared = input_rows(key)
    return shared.astype(jnp.bfloat16)


def draw_router(key, part):
    key = jax.random.fold_in(key, 5)
    base = jax.random.normal(key, (D, EXPERTS), jnp.float32) * (1.5 / math.sqrt(D))
    return base.astype(jnp.bfloat16)


def levels(stream_key, shape, cuts, low, largest):
    level = 1.0
    for dim, shards_of in cuts:
        heights = jax.random.uniform(jax.random.fold_in(jax.random.fold_in(stream_key, 6), dim), (shards_of,), jnp.float32, low / len(cuts), largest / len(cuts))
        level = level * jnp.repeat(jnp.exp(heights), shape[dim] // shards_of).reshape((-1,) + (1,) * (len(shape) - 1 - dim))
    return level


def bell_draw(key, extent, scale, reach, cuts=(), held_as=jnp.bfloat16):
    entries = jax.random.normal(key, extent, jnp.float32) * scale
    if len(cuts) > 0:
        entries = levels(key, extent, cuts, -0.22, 0.18) * entries
    return jnp.clip(entries, min=-reach, max=reach).astype(held_as)


def setup_inputs(seed: int = 0) -> dict:
    key_of = jax.random.split(jax.random.key(seed), 8)
    return {
        "inputs": draw_inputs(jax.random.fold_in(key_of[7], 71), 0),
        "cotangent": bell_draw(key_of[1], (TOKENS, D), 0.5, 4.0, ((0, 256),)),
        "routes": draw_routes(jax.random.fold_in(key_of[7], 71), 0),
        "router": draw_router(jax.random.fold_in(key_of[7], 71), 0),
        "w_gate": bell_draw(key_of[4], (EXPERTS, D, FF), D ** -0.5, 0.125, ((0, 64),)),
        "w_up": bell_draw(key_of[5], (EXPERTS, D, FF), D ** -0.5, 0.125, ((0, 64),)),
        "w_down": bell_draw(key_of[6], (EXPERTS, FF, D), FF ** -0.5, 0.3125, ((0, 64),)),
    }


def forward_rows(gate_w, up_w, down_w, rows_in):
    gate = jnp.dot(rows_in, gate_w, preferred_element_type=jnp.float32)
    up = jnp.dot(rows_in, up_w, preferred_element_type=jnp.float32)
    sig = jax.nn.sigmoid(gate)
    act = gate * sig
    hidden = (act * up).astype(jnp.bfloat16)
    out = jnp.dot(hidden, down_w, preferred_element_type=jnp.float32)
    return gate, up, sig, act, out


def backward_rows(gate_w, up_w, down_w, saved, rows_cot, comb_rows):
    gate, up, sig, act, out = saved
    cot = rows_cot.astype(jnp.float32)
    dcomb = jnp.sum(out * cot, axis=-1).astype(jnp.bfloat16)
    scaled = (comb_rows.astype(jnp.float32)[:, None] * cot).astype(jnp.bfloat16)
    dims = (((1,), (1,)), ((), ()))
    dhid = lax.dot_general(scaled, down_w, dims, preferred_element_type=jnp.float32)
    dgate = (dhid * up * sig * (1.0 + gate * (1.0 - sig))).astype(jnp.bfloat16)
    dup = (dhid * act).astype(jnp.bfloat16)
    dpart = lax.dot_general(dgate, gate_w, dims, preferred_element_type=jnp.float32)
    dpart = dpart + lax.dot_general(dup, up_w, dims, preferred_element_type=jnp.float32)
    return dpart.astype(jnp.bfloat16), dcomb


def reference(inputs, cotangent, routes, router, w_gate, w_up, w_down):
    count_tok = inputs.shape[0]
    logits = jnp.dot(inputs, router, preferred_element_type=jnp.float32)
    chosen = jnp.take_along_axis(logits, routes, axis=1)
    top = jnp.max(chosen, axis=1, keepdims=True)
    expo = jnp.exp(chosen - top)
    combine = expo / jnp.sum(expo, axis=1, keepdims=True)
    comb_flat = combine.astype(jnp.bfloat16).reshape(-1)
    flat = routes.reshape(-1).astype(jnp.int32)
    total = flat.shape[0]
    order = jnp.argsort(flat, stable=True).astype(jnp.int32)
    counts = jnp.zeros((EXPERTS,), jnp.int32).at[flat].add(1)
    block = 512
    padded = ((counts + block - 1) // block) * block
    pstart = (jnp.cumsum(padded) - padded).astype(jnp.int32)
    start = (jnp.cumsum(counts) - counts).astype(jnp.int32)
    nblocks = (total + block - 1) // block + EXPERTS
    lanes = jnp.arange(block, dtype=jnp.int32)

    def step(carry, index):
        accum, dcs = carry
        pos = index * block
        expert = jnp.clip(jnp.sum((pstart <= pos).astype(jnp.int32)) - 1, 0, EXPERTS - 1).astype(jnp.int32)
        local = pos - pstart[expert] + lanes
        valid = local < counts[expert]
        picked = jnp.clip(start[expert] + local, 0, total - 1).astype(jnp.int32)
        row = order[picked]
        token = row // TOPK
        weights = (w_gate[expert], w_up[expert], w_down[expert])
        saved = forward_rows(weights[0], weights[1], weights[2], inputs[token])
        dpart, dcomb = backward_rows(weights[0], weights[1], weights[2], saved, cotangent[token], comb_flat[row])
        accum = accum.at[token].add(jnp.where(valid[:, None], dpart.astype(jnp.float32), jnp.float32(0.0)))
        dcs = dcs.at[row].add(jnp.where(valid, dcomb.astype(jnp.float32), jnp.float32(0.0)))
        return (accum, dcs), None

    init = (jnp.zeros((count_tok, D), jnp.float32), jnp.zeros((total,), jnp.float32))
    (accum, dcs), _ = lax.scan(step, init, jnp.arange(nblocks, dtype=jnp.int32))
    dcomb = dcs.reshape(count_tok, TOPK)
    dlogit = combine * (dcomb - jnp.sum(combine * dcomb, axis=1, keepdims=True))
    member = (routes[:, :, None] == jnp.arange(EXPERTS, dtype=jnp.int32)[None, None, :]).astype(jnp.float32)
    spread = jnp.sum(dlogit[:, :, None] * member, axis=1).astype(jnp.bfloat16)
    back = lax.dot_general(spread, router, (((1,), (1,)), ((), ())), preferred_element_type=jnp.float32)
    grad_inputs = (accum + back).astype(jnp.bfloat16)
    grad_router = lax.dot_general(inputs, spread, (((0,), (0,)), ((), ())), preferred_element_type=jnp.float32)
    return grad_inputs, grad_router
```

```python
import jax
import jax.numpy as jnp
from jax import lax
from jax.sharding import Mesh, PartitionSpec as P

NZ, NY, NC, NX = 8, 4, 2, 4
SLICE = NY * NC
EXPERTS = NZ * SLICE
CAP = 16
HOT = 2
HOT_CAP = 64
BF = jnp.bfloat16
F32 = jnp.float32
ROWS = ("z", "y", "c", "x")
GROUP = ("z", "y", "c")
PLANE = ("y", "c")


def exchange(value, axes):
    return lax.all_to_all(value, axes, split_axis=0, concat_axis=0, tiled=True)


def spread_out(value, axes, count):
    return exchange(jnp.broadcast_to(value[None], (count,) + value.shape), axes)


def dot(a, b, dims):
    return lax.dot_general(a, b, (dims, ((), ())), preferred_element_type=F32)


def selectors(code, weight, slots):
    ids = lax.broadcasted_iota(jnp.int32, (1, slots, 1), 1)
    hits = code[:, :, None, :] == ids[:, None]
    chosen = jnp.sum(hits.astype(F32), axis=1).astype(BF)
    weighted = jnp.sum(jnp.where(hits, weight[:, :, None, :], 0.0), axis=1).astype(BF)
    return chosen, weighted


def around(value, axis, size):
    turned = [value] + [
        lax.ppermute(value, axis, [(i, (i - shift) % size) for i in range(size)])
        for shift in range(1, size)
    ]
    return jnp.roll(jnp.stack(turned), lax.axis_index(axis), axis=0)


def earlier(count):
    size = count.shape[-1]
    rows = lax.broadcasted_iota(jnp.int32, (size, size), 0)
    cols = lax.broadcasted_iota(jnp.int32, (size, size), 1)
    mask = (rows < cols).astype(BF)
    before = lax.dot_general(
        count.astype(BF), mask, (((count.ndim - 1,), (0,)), ((), ())), preferred_element_type=F32
    )
    return before.astype(jnp.int32)


def forward(gate, up):
    sig = jax.nn.sigmoid(gate)
    act = gate * sig
    slope = up * sig * (1.0 + gate * (1.0 - sig))
    return lax.reduce_precision(act * up, 8, 7), act, slope


def backward(saved, dhid):
    hidden, act, slope = saved
    dcomb = lax.reduce_precision(jnp.sum(hidden * dhid, axis=-1), 8, 7)
    return (dhid * slope).astype(BF), (dhid * act).astype(BF), dcomb


def hot_expert(rows_in, rows_cot, mine, other, side):
    half = rows_in.shape[1] // 2
    ff = mine.shape[1] // 3

    def halves(rows):
        low, high = rows[:, :half], rows[:, half:]
        return jnp.where(side == 0, low, high), jnp.where(side == 0, high, low)

    in_mine, in_other = halves(rows_in)
    cot_mine, cot_other = halves(rows_cot)
    both = dot(in_mine, mine[:, : 2 * ff], ((1,), (0,))) + dot(
        in_other, other[:, : 2 * ff], ((1,), (0,))
    )
    saved = forward(both[:, :ff], both[:, ff:])
    dhid = dot(cot_mine, mine[:, 2 * ff :], ((1,), (0,))) + dot(
        cot_other, other[:, 2 * ff :], ((1,), (0,))
    )
    dgate, dup, dcomb = backward(saved, dhid)
    grads = jnp.concatenate([dgate, dup], axis=1)
    dx_mine = dot(grads, mine[:, : 2 * ff], ((1,), (1,))).astype(BF)
    dx_other = dot(grads, other[:, : 2 * ff], ((1,), (1,))).astype(BF)
    low = jnp.where(side == 0, dx_mine, dx_other)
    high = jnp.where(side == 0, dx_other, dx_mine)
    return jnp.concatenate([low, high], axis=1), dcomb


def shards(inputs, cotangent, routes, router, w_gate, w_up, w_down):
    tok, width = inputs.shape
    topk = routes.shape[1]
    zi, ci, xi = lax.axis_index("z"), lax.axis_index("c"), lax.axis_index("x")
    rows = SLICE * NZ * CAP

    routes_t = routes.T
    in_all = lax.all_gather(inputs, "z")

    part = width // (NC * NZ * NY * NX)

    def quarter(weights):
        blocks = weights.reshape(NC, NZ, NY, NX, part, weights.shape[1])
        return lax.dynamic_index_in_dim(blocks, xi, axis=3, keepdims=False)

    packed = jnp.concatenate([quarter(w_gate[0]), quarter(w_up[0]), quarter(w_down[0].T)], axis=-1)
    cols = packed.shape[-1]
    pieces = exchange(packed.transpose(2, 0, 1, 3, 4).reshape(SLICE, NZ, part, cols), PLANE)

    member = routes_t[:, None, :] == lax.broadcasted_iota(jnp.int32, (1, EXPERTS, 1), 1)
    member_f = member.astype(F32)
    count = jnp.sum(member.astype(jnp.int32), axis=0)
    before = earlier(count)
    is_hot = (jnp.sum(count, axis=1) > CAP).astype(jnp.int32)
    ids = jnp.arange(EXPERTS, dtype=jnp.int32)
    hot_rank = jnp.sum(jnp.where(ids[None, :] < ids[:, None], is_hot[None, :], 0), axis=1)
    hot_pick = is_hot[None, :] * (hot_rank[None, :] == jnp.arange(HOT)[:, None]).astype(jnp.int32)
    hot_id = jnp.sum(hot_pick * ids[None, :], axis=1)
    ks = jnp.arange(topk)
    same = (routes_t[:, None, :] == routes_t[None, :, :]) & (ks[None, :] < ks[:, None])[:, :, None]
    rank = jnp.sum(jnp.where(member, before[None], 0), axis=1) + jnp.sum(same.astype(jnp.int32), axis=1)
    hot_slot = jnp.sum(jnp.where(routes_t[None] == hot_id[:, None, None], 1 + jnp.arange(HOT)[:, None, None], 0), axis=0)
    code = jnp.where(hot_slot > 0, -1, routes_t * CAP + rank)
    hot_code = jnp.where(hot_slot > 0, (hot_slot - 1) * HOT_CAP + rank, -1)
    logits = dot(router, inputs, ((0,), (1,)))
    chosen = jnp.sum(logits[None] * member_f, axis=1)
    expo = jnp.exp(chosen - jnp.max(chosen, axis=0, keepdims=True))
    combine = expo / jnp.sum(expo, axis=0, keepdims=True)
    comb_sent = combine.astype(BF).astype(F32)

    ring = spread_out(jnp.concatenate([code.astype(F32), comb_sent], axis=0), "z", NZ)
    local = ring[:, :topk].astype(jnp.int32) - zi * SLICE * CAP
    pick, pick_comb = selectors(local, ring[:, topk:], SLICE * CAP)
    hot_ids = [hot_id] + [
        lax.ppermute(hot_id, "x", [(i, (i - shift) % NX) for i in range(NX)]) for shift in range(1, NX)
    ]
    in_all, pick, pieces, hot_ids, later_cot = lax.optimization_barrier(
        (in_all, pick, pieces, hot_ids, cotangent)
    )
    cot_all = lax.all_gather(later_cot, "z")

    sources = zi * SLICE + jnp.arange(SLICE)
    got = []
    for shift in range(NX):
        wanted = (sources[None, :] == hot_ids[shift][:, None])[:, :, None, None, None]
        held = jnp.sum(jnp.where(wanted, pieces[None], jnp.zeros((), BF)), axis=1, dtype=BF)
        if shift:
            held = lax.ppermute(held, "x", [(i, (i + shift) % NX) for i in range(NX)])
        got.append(held)
    quarters = jnp.roll(jnp.stack([got[-j % NX] for j in range(NX)]), xi, axis=0)
    held = quarters.transpose(2, 1, 0, 3, 4).reshape(NZ, HOT * NX * part, cols)

    def to_experts(all_rows):
        sent = lax.dot_general(pick, all_rows, (((2,), (1,)), ((0,), (0,))), preferred_element_type=F32)
        sent = sent.astype(BF).reshape(NZ, SLICE, CAP, width).transpose(1, 0, 2, 3)
        return exchange(sent, PLANE).reshape(rows, width)

    rows_in = to_experts(in_all)
    rows_in, held, cot_all = lax.optimization_barrier((rows_in, held, cot_all))
    rows_cot = to_experts(cot_all)
    held = lax.psum_scatter(held, "z", scatter_dimension=0).reshape(HOT, NX * part, cols)
    held = around(held, "y", NY).transpose(1, 0, 2, 3).reshape(HOT, NY * NX * part, cols)
    saved = forward(dot(rows_in, w_gate[0], ((1,), (0,))), dot(rows_in, w_up[0], ((1,), (0,))))
    rows_cot, saved, held = lax.optimization_barrier((rows_cot, saved, held))
    dgate, dup, dcomb_rows = backward(saved, dot(rows_cot, w_down[0], ((1,), (1,))))
    dpart = dot(dgate, w_gate[0], ((1,), (1,))) + dot(dup, w_up[0], ((1,), (1,)))
    dpart = dpart.astype(BF)
    dcomb_rows = dcomb_rows.reshape(SLICE, NZ, CAP).transpose(1, 0, 2).reshape(EXPERTS, CAP)
    dcomb_rows = jnp.pad(dcomb_rows, ((0, 0), (0, 128 - CAP))).reshape(EXPERTS, 1, 128)
    dcomb_slots = exchange(dcomb_rows, GROUP)
    dpart, dcomb_slots = lax.optimization_barrier((dpart, dcomb_slots))

    mine = lax.all_gather(held, "z", axis=1, tiled=True)
    back_rows = exchange(dpart.reshape(SLICE, NZ, CAP, width), PLANE)
    back_rows, mine = lax.optimization_barrier((back_rows, mine))
    other = lax.ppermute(mine, "c", [(0, 1), (1, 0)])
    hot_rows, hot_rows_comb = selectors(hot_code[None], comb_sent[None], HOT * HOT_CAP)
    hot_in = dot(hot_rows[0], inputs, ((1,), (0,))).astype(BF).reshape(HOT, HOT_CAP, width)
    hot_cot = dot(hot_rows[0], cotangent, ((1,), (0,))).astype(BF).reshape(HOT, HOT_CAP, width)
    hot_dx, hot_dcomb = [], []
    for index in range(HOT):
        dx, dcomb = hot_expert(hot_in[index], hot_cot[index], mine[index], other[index], ci)
        hot_dx.append(dx)
        hot_dcomb.append(dcomb)
    hot_grad = dot(hot_rows_comb[0], jnp.concatenate(hot_dx, axis=0), ((0,), (0,)))

    back_rows = back_rows.transpose(1, 0, 2, 3).reshape(NZ, SLICE * CAP, width)
    partial = lax.dot_general(
        pick_comb, back_rows, (((1,), (1,)), ((0,), (0,))), preferred_element_type=F32
    )
    cold_grad = lax.psum_scatter(partial.astype(BF), "z", scatter_dimension=0)

    hot_pick_f = hot_pick.astype(F32)
    cold = 1.0 - jnp.sum(hot_pick_f, axis=0)
    dcomb_slots = dcomb_slots[:, 0, :HOT_CAP] * cold[:, None]
    dcomb_slots = dcomb_slots + jnp.sum(
        hot_pick_f[:, :, None] * jnp.stack(hot_dcomb)[:, None, :], axis=0
    )
    by_rank = lax.dot_general(
        member.astype(BF), dcomb_slots.astype(BF), (((1,), (0,)), ((), ())), preferred_element_type=F32
    )
    ranked = rank[:, None, :] == lax.broadcasted_iota(jnp.int32, (1, HOT_CAP, 1), 1)
    dcomb = jnp.sum(jnp.where(ranked, by_rank.transpose(0, 2, 1), 0.0), axis=1)
    dlogit = combine * (dcomb - jnp.sum(combine * dcomb, axis=0, keepdims=True))
    spread = jnp.sum(dlogit[:, None, :] * member_f, axis=0).astype(BF)
    devices = NZ * NY * NC * NX
    local_router = dot(spread, inputs, ((1,), (0,)))
    lanes = EXPERTS * width // (devices * 4)
    shares = exchange(local_router.reshape(devices, 4, lanes), ROWS)
    total = jnp.sum(shares, axis=0)
    grad_router = spread_out(total, ROWS, devices).reshape(EXPERTS, width).T

    back = dot(spread, router, ((0,), (1,)))
    grad_inputs = (cold_grad.astype(F32) + hot_grad + back).astype(BF)
    return grad_inputs, grad_router


def solution(mesh):
    fine = Mesh(mesh.devices.reshape(NZ, NY, NC, NX), ROWS)
    tokens = P(ROWS, None)
    experts = P(GROUP, None, None)
    return jax.shard_map(
        shards,
        mesh=fine,
        in_specs=(tokens, tokens, tokens, P(), experts, experts, experts),
        out_specs=(tokens, P()),
        check_vma=False,
    )
```

```python
import jax
import jax.numpy as jnp
from jax import lax
from jax.experimental import pallas as pl
from jax.experimental.pallas import tpu as pltpu
from jax.sharding import Mesh, PartitionSpec as P

NZ, NY, NC, NX = 8, 4, 2, 4
SLICE = NY * NC
EXPERTS = NZ * SLICE
CAP = 16
HOT = 2
HOT_CAP = 64
ORDER = (4, 3, 5, 2, 6, 1, 7, 0)
FAR = 3
BF = jnp.bfloat16
F32 = jnp.float32
ROWS = ("z", "y", "c", "x")
GROUP = ("z", "y", "c")
PLANE = ("y", "c")


def exchange(value, axes):
    return lax.all_to_all(value, axes, split_axis=0, concat_axis=0, tiled=True)


def spread_out(value, axes, count):
    return exchange(jnp.broadcast_to(value[None], (count,) + value.shape), axes)


def dot(a, b, dims):
    return lax.dot_general(a, b, (dims, ((), ())), preferred_element_type=F32)


def selectors(code, weight, slots):
    ids = lax.broadcasted_iota(jnp.int32, (1, slots, 1), 1)
    hits = code[:, :, None, :] == ids[:, None]
    chosen = jnp.sum(hits.astype(F32), axis=1).astype(BF)
    weighted = jnp.sum(jnp.where(hits, weight[:, :, None, :], 0.0), axis=1).astype(BF)
    return chosen, weighted


def slot_hits(code, slots):
    ids = lax.broadcasted_iota(jnp.int32, (slots, code.shape[-1]), 0)
    return [code[k : k + 1] == ids for k in range(code.shape[0])]


def gather_kernel(index_ref, code_ref, rows_ref, out_ref, rows, sent, in_sems, out_sems):
    def incoming(i):
        return pltpu.make_async_copy(rows_ref.at[index_ref[i]], rows.at[i], in_sems.at[i])

    def outgoing(i):
        return pltpu.make_async_copy(sent.at[i], out_ref.at[:, i], out_sems.at[i])

    for i in range(NZ):
        incoming(i).start()
    for i in range(NZ):
        hits = slot_hits(code_ref[index_ref[i]], SLICE * CAP)
        pick = sum(jnp.where(hit, 1.0, 0.0) for hit in hits).astype(BF)
        incoming(i).wait()
        chosen = jnp.dot(pick, rows[i], preferred_element_type=F32).astype(BF)
        sent[i] = chosen.reshape(SLICE, CAP, chosen.shape[-1])
        outgoing(i).start()
    for i in range(NZ):
        outgoing(i).wait()


def gather(index, code, all_rows):
    tok, width = all_rows.shape[1:]
    return pl.pallas_call(
        gather_kernel,
        in_specs=[
            pl.BlockSpec(memory_space=pltpu.SMEM),
            pl.BlockSpec(memory_space=pltpu.VMEM),
            pl.BlockSpec(memory_space=pl.ANY),
        ],
        out_specs=pl.BlockSpec(memory_space=pl.ANY),
        scratch_shapes=[
            pltpu.VMEM((NZ, tok, width), BF),
            pltpu.VMEM((NZ, SLICE, CAP, width), BF),
            pltpu.SemaphoreType.DMA((NZ,)),
            pltpu.SemaphoreType.DMA((NZ,)),
        ],
        out_shape=jax.ShapeDtypeStruct((SLICE, NZ, CAP, width), BF),
        compiler_params=pltpu.CompilerParams(vmem_limit_bytes=56 * 1024 * 1024),
        cost_estimate=pl.CostEstimate(
            flops=2 * NZ * SLICE * CAP * tok * width,
            bytes_accessed=4 * NZ * tok * width,
            transcendentals=0,
        ),
        name="gather_rows",
    )(index, code, all_rows)


def combine_kernel(index_ref, code_ref, comb_ref, rows_ref, *refs):
    *carried, out_ref = refs
    comb = comb_ref[0]
    hits = slot_hits(code_ref[0], SLICE * CAP)
    weights = sum(jnp.where(hit, comb[k : k + 1], 0.0) for k, hit in enumerate(hits))
    rows = rows_ref[:, 0].reshape(SLICE * CAP, rows_ref.shape[-1])
    dims = (((0,), (0,)), ((), ()))
    total = lax.dot_general(weights.astype(BF), rows, dims, preferred_element_type=F32)
    out_ref[0] = total.astype(BF)
    for step, carry_ref in enumerate(carried):

        @pl.when(pl.program_id(0) == step)
        def _():
            out_ref[0] = (total + carry_ref[...].astype(F32)).astype(BF)


def combine_rows(index, code, comb, rows, first, count, *carried):
    topk, tok = code.shape[1:]
    width = rows.shape[3]
    tokens = pl.BlockSpec((1, topk, tok), lambda i, index: (index[i], 0, 0))
    return pl.pallas_call(
        combine_kernel,
        grid_spec=pltpu.PrefetchScalarGridSpec(
            num_scalar_prefetch=1,
            grid=(count,),
            in_specs=[
                tokens,
                tokens,
                pl.BlockSpec((SLICE, 1, CAP, width), lambda i, index: (0, i + first, 0, 0)),
            ]
            + [pl.BlockSpec((tok, width), lambda i, index: (0, 0)) for _ in carried],
            out_specs=pl.BlockSpec((1, tok, width), lambda i, index: (i, 0, 0)),
        ),
        out_shape=jax.ShapeDtypeStruct((count, tok, width), BF),
        compiler_params=pltpu.CompilerParams(vmem_limit_bytes=32 * 1024 * 1024),
        cost_estimate=pl.CostEstimate(
            flops=2 * count * SLICE * CAP * tok * width,
            bytes_accessed=4 * count * tok * width,
            transcendentals=0,
        ),
        name="combine_rows",
    )(index, code, comb, rows, *carried)


def around(value, axis, size):
    turned = [value] + [
        lax.ppermute(value, axis, [(i, (i - shift) % size) for i in range(size)])
        for shift in range(1, size)
    ]
    return jnp.roll(jnp.stack(turned), lax.axis_index(axis), axis=0)


def earlier(count):
    size = count.shape[-1]
    rows = lax.broadcasted_iota(jnp.int32, (size, size), 0)
    cols = lax.broadcasted_iota(jnp.int32, (size, size), 1)
    mask = (rows < cols).astype(BF)
    before = lax.dot_general(
        count.astype(BF), mask, (((count.ndim - 1,), (0,)), ((), ())), preferred_element_type=F32
    )
    return before.astype(jnp.int32)


def forward(gate, up):
    sig = jax.nn.sigmoid(gate)
    act = gate * sig
    slope = up * sig * (1.0 + gate * (1.0 - sig))
    return lax.reduce_precision(act * up, 8, 7), act, slope


def backward(saved, dhid):
    hidden, act, slope = saved
    dcomb = lax.reduce_precision(jnp.sum(hidden * dhid, axis=-1), 8, 7)
    return (dhid * slope).astype(BF), (dhid * act).astype(BF), dcomb


def hot_expert(rows_in, rows_cot, mine, other, side):
    half = rows_in.shape[1] // 2
    ff = mine.shape[1] // 3

    def halves(rows):
        low, high = rows[:, :half], rows[:, half:]
        return jnp.where(side == 0, low, high), jnp.where(side == 0, high, low)

    in_mine, in_other = halves(rows_in)
    cot_mine, cot_other = halves(rows_cot)
    both = dot(in_mine, mine[:, : 2 * ff], ((1,), (0,))) + dot(
        in_other, other[:, : 2 * ff], ((1,), (0,))
    )
    saved = forward(both[:, :ff], both[:, ff:])
    dhid = dot(cot_mine, mine[:, 2 * ff :], ((1,), (0,))) + dot(
        cot_other, other[:, 2 * ff :], ((1,), (0,))
    )
    dgate, dup, dcomb = backward(saved, dhid)
    grads = jnp.concatenate([dgate, dup], axis=1)
    dx_mine = dot(grads, mine[:, : 2 * ff], ((1,), (1,))).astype(BF)
    dx_other = dot(grads, other[:, : 2 * ff], ((1,), (1,))).astype(BF)
    low = jnp.where(side == 0, dx_mine, dx_other)
    high = jnp.where(side == 0, dx_other, dx_mine)
    return jnp.concatenate([low, high], axis=1), dcomb


def shards(inputs, cotangent, routes, router, w_gate, w_up, w_down):
    tok, width = inputs.shape
    topk = routes.shape[1]
    zi, ci, xi = lax.axis_index("z"), lax.axis_index("c"), lax.axis_index("x")
    rows = SLICE * NZ * CAP

    routes_t = routes.T
    in_all = lax.all_gather(inputs, "z")

    part = width // (NC * NZ * NY * NX)

    def quarter(weights):
        blocks = weights.reshape(NC, NZ, NY, NX, part, weights.shape[1])
        return lax.dynamic_index_in_dim(blocks, xi, axis=3, keepdims=False)

    packed = jnp.concatenate([quarter(w_gate[0]), quarter(w_up[0]), quarter(w_down[0].T)], axis=-1)
    cols = packed.shape[-1]
    pieces = exchange(packed.transpose(2, 0, 1, 3, 4).reshape(SLICE, NZ, part, cols), PLANE)

    member = routes_t[:, None, :] == lax.broadcasted_iota(jnp.int32, (1, EXPERTS, 1), 1)
    member_f = member.astype(F32)
    count = jnp.sum(member.astype(jnp.int32), axis=0)
    before = earlier(count)
    is_hot = (jnp.sum(count, axis=1) > CAP).astype(jnp.int32)
    ids = jnp.arange(EXPERTS, dtype=jnp.int32)
    hot_rank = jnp.sum(jnp.where(ids[None, :] < ids[:, None], is_hot[None, :], 0), axis=1)
    hot_pick = is_hot[None, :] * (hot_rank[None, :] == jnp.arange(HOT)[:, None]).astype(jnp.int32)
    hot_id = jnp.sum(hot_pick * ids[None, :], axis=1)
    ks = jnp.arange(topk)
    same = (routes_t[:, None, :] == routes_t[None, :, :]) & (ks[None, :] < ks[:, None])[:, :, None]
    rank = jnp.sum(jnp.where(member, before[None], 0), axis=1) + jnp.sum(same.astype(jnp.int32), axis=1)
    hot_slot = jnp.sum(jnp.where(routes_t[None] == hot_id[:, None, None], 1 + jnp.arange(HOT)[:, None, None], 0), axis=0)
    code = jnp.where(hot_slot > 0, -1, routes_t * CAP + rank)
    hot_code = jnp.where(hot_slot > 0, (hot_slot - 1) * HOT_CAP + rank, -1)
    logits = dot(router, inputs, ((0,), (1,)))
    chosen = jnp.sum(logits[None] * member_f, axis=1)
    expo = jnp.exp(chosen - jnp.max(chosen, axis=0, keepdims=True))
    combine = expo / jnp.sum(expo, axis=0, keepdims=True)
    comb_sent = combine.astype(BF).astype(F32)

    ring = spread_out(jnp.concatenate([code.astype(F32), comb_sent], axis=0), "z", NZ)
    local = ring[:, :topk].astype(jnp.int32) - zi * SLICE * CAP
    comb_all = ring[:, topk:]
    index = (zi + jnp.array(ORDER, jnp.int32)) % NZ
    hot_ids = [hot_id] + [
        lax.ppermute(hot_id, "x", [(i, (i - shift) % NX) for i in range(NX)]) for shift in range(1, NX)
    ]
    sources = zi * SLICE + jnp.arange(SLICE)
    picked = []
    for shift in range(NX):
        wanted = (sources[None, :] == hot_ids[shift][:, None])[:, :, None, None, None]
        picked.append(jnp.sum(jnp.where(wanted, pieces[None], jnp.zeros((), BF)), axis=1, dtype=BF))
    in_all, local, picked, later_cot = lax.optimization_barrier((in_all, local, picked, cotangent))
    cot_all = lax.all_gather(later_cot, "z")
    got = [picked[0]] + [
        lax.ppermute(picked[shift], "x", [(i, (i + shift) % NX) for i in range(NX)])
        for shift in range(1, NX)
    ]
    quarters = jnp.roll(jnp.stack([got[-j % NX] for j in range(NX)]), xi, axis=0)
    held = quarters.transpose(2, 1, 0, 3, 4).reshape(NZ, HOT * NX * part, cols)
    rows_in = exchange(gather(index, local, in_all), PLANE).reshape(rows, width)
    sent_cot = gather(index, local, cot_all)
    rows_in, sent_cot, held = lax.optimization_barrier((rows_in, sent_cot, held))
    rows_cot = exchange(sent_cot, PLANE).reshape(rows, width)
    held = lax.psum_scatter(held, "z", scatter_dimension=0).reshape(HOT, NX * part, cols)
    held = around(held, "y", NY).transpose(1, 0, 2, 3).reshape(HOT, NY * NX * part, cols)
    saved = forward(dot(rows_in, w_gate[0], ((1,), (0,))), dot(rows_in, w_up[0], ((1,), (0,))))
    rows_cot, saved, held = lax.optimization_barrier((rows_cot, saved, held))
    dgate, dup, dcomb_rows = backward(saved, dot(rows_cot, w_down[0], ((1,), (1,))))

    def input_grads(part_rows):
        def of(rows_of):
            return rows_of.reshape(SLICE, NZ, CAP, -1)[:, part_rows].reshape(-1, rows_of.shape[1])

        grads = dot(of(dgate), w_gate[0], ((1,), (1,))) + dot(of(dup), w_up[0], ((1,), (1,)))
        return grads.astype(BF).reshape(SLICE, -1, CAP, width)

    dpart_far, dpart_near = input_grads(slice(0, FAR)), input_grads(slice(FAR, NZ))
    dcomb_rows = dcomb_rows.reshape(SLICE, NZ, CAP).transpose(1, 0, 2).reshape(NZ, SLICE * CAP)
    placed = (index[None, :] == jnp.arange(NZ)[:, None]).astype(BF)
    dcomb_rows = dot(placed, dcomb_rows.astype(BF), ((1,), (0,))).reshape(EXPERTS, CAP)
    dcomb_rows = jnp.pad(dcomb_rows, ((0, 0), (0, 128 - CAP))).reshape(EXPERTS, 1, 128)
    dcomb_slots = exchange(dcomb_rows, GROUP)
    dpart_far, dpart_near, dcomb_slots = lax.optimization_barrier((dpart_far, dpart_near, dcomb_slots))

    def up_ring(value):
        return lax.ppermute(value, "z", [(i, (i + 1) % NZ) for i in range(NZ)])

    def down_ring(value):
        return lax.ppermute(value, "z", [(i, (i - 1) % NZ) for i in range(NZ)])

    def added(first, second):
        return (first.astype(F32) + second.astype(F32)).astype(BF)

    back_far = exchange(dpart_far, PLANE)
    back_far, dpart_near = lax.optimization_barrier((back_far, dpart_near))
    back_near = exchange(dpart_near, PLANE)
    far = combine_rows(index[:FAR], local, comb_all, back_far, 0, FAR)
    rising = up_ring(added(up_ring(far[0]), far[1]))
    falling = down_ring(far[2])

    mine = lax.all_gather(held, "z", axis=1, tiled=True)
    other = lax.ppermute(mine, "c", [(0, 1), (1, 0)])
    hot_rows, hot_rows_comb = selectors(hot_code[None], comb_sent[None], HOT * HOT_CAP)
    hot_in = dot(hot_rows[0], inputs, ((1,), (0,))).astype(BF).reshape(HOT, HOT_CAP, width)
    hot_cot = dot(hot_rows[0], cotangent, ((1,), (0,))).astype(BF).reshape(HOT, HOT_CAP, width)
    hot_dx, hot_dcomb = [], []
    for slot in range(HOT):
        dx, dcomb = hot_expert(hot_in[slot], hot_cot[slot], mine[slot], other[slot], ci)
        hot_dx.append(dx)
        hot_dcomb.append(dcomb)
    hot_grad = dot(hot_rows_comb[0], jnp.concatenate(hot_dx, axis=0), ((0,), (0,)))

    hot_pick_f = hot_pick.astype(F32)
    cold = 1.0 - jnp.sum(hot_pick_f, axis=0)
    dcomb_slots = dcomb_slots[:, 0, :HOT_CAP] * cold[:, None]
    dcomb_slots = dcomb_slots + jnp.sum(
        hot_pick_f[:, :, None] * jnp.stack(hot_dcomb)[:, None, :], axis=0
    )
    by_rank = lax.dot_general(
        member.astype(BF), dcomb_slots.astype(BF), (((1,), (0,)), ((), ())), preferred_element_type=F32
    )
    ranked = rank[:, None, :] == lax.broadcasted_iota(jnp.int32, (1, HOT_CAP, 1), 1)
    dcomb = jnp.sum(jnp.where(ranked, by_rank.transpose(0, 2, 1), 0.0), axis=1)
    dlogit = combine * (dcomb - jnp.sum(combine * dcomb, axis=0, keepdims=True))
    spread = jnp.sum(dlogit[:, None, :] * member_f, axis=0).astype(BF)
    local_router = dot(spread, inputs, ((1,), (0,))).reshape(NX, EXPERTS // NX, width)
    local_router = jnp.roll(local_router, -xi, axis=0)
    local_router = local_router[0] + sum(
        lax.ppermute(local_router[shift], "x", [(i, (i + shift) % NX) for i in range(NX)])
        for shift in range(1, NX)
    )
    back_near, rising, falling, local_router, hot_grad, spread = lax.optimization_barrier(
        (back_near, rising, falling, local_router, hot_grad, spread)
    )
    near_ids = index[FAR:]
    second = combine_rows(near_ids[:2], local, comb_all, back_near, 0, 2, rising, falling)
    rising, falling = up_ring(second[0]), down_ring(second[1])
    third = combine_rows(near_ids[2:4], local, comb_all, back_near, 2, 2, rising, falling)
    rising, falling = up_ring(third[0]), down_ring(third[1])
    own = combine_rows(near_ids[4:], local, comb_all, back_near, 4, 1)[0]

    lanes = local_router.size // (SLICE * CAP)
    shares = exchange(local_router.reshape(SLICE, CAP, lanes), PLANE)
    shares = spread_out(jnp.sum(shares, axis=0), "z", NZ)
    shares = spread_out(jnp.sum(shares, axis=0), PLANE, SLICE).reshape(EXPERTS // NX, width)
    grad_router = around(shares, "x", NX).reshape(EXPERTS, width).T

    back = dot(spread, router, ((0,), (1,)))
    grad_inputs = (own.astype(F32) + rising.astype(F32) + falling.astype(F32) + hot_grad + back).astype(BF)
    return grad_inputs, grad_router


def solution(mesh):
    fine = Mesh(mesh.devices.reshape(NZ, NY, NC, NX), ROWS)
    tokens = P(ROWS, None)
    experts = P(GROUP, None, None)
    return jax.shard_map(
        shards,
        mesh=fine,
        in_specs=(tokens, tokens, tokens, P(), experts, experts, experts),
        out_specs=(tokens, P()),
        check_vma=False,
    )
```

```python
import jax
import jax.numpy as jnp
from jax import lax
from jax.experimental import pallas as pl
from jax.experimental.pallas import tpu as pltpu
from jax.sharding import Mesh, PartitionSpec as P

NZ, NY, NC, NX = 8, 4, 2, 4
SLICE = NY * NC
EXPERTS = NZ * SLICE
CAP = 16
HOT = 2
HOT_CAP = 64
ORDER = (4, 3, 5, 2, 6, 1, 7, 0)
FAR = 4
BF = jnp.bfloat16
F32 = jnp.float32
ROWS = ("z", "y", "c", "x")
GROUP = ("z", "y", "c")
PLANE = ("y", "c")


def exchange(value, axes):
    return lax.all_to_all(value, axes, split_axis=0, concat_axis=0, tiled=True)


def spread_out(value, axes, count):
    return exchange(jnp.broadcast_to(value[None], (count,) + value.shape), axes)


def dot(a, b, dims):
    return lax.dot_general(a, b, (dims, ((), ())), preferred_element_type=F32)


def selectors(code, weight, slots):
    ids = lax.broadcasted_iota(jnp.int32, (1, slots, 1), 1)
    hits = code[:, :, None, :] == ids[:, None]
    chosen = jnp.sum(hits.astype(F32), axis=1).astype(BF)
    weighted = jnp.sum(jnp.where(hits, weight[:, :, None, :], 0.0), axis=1).astype(BF)
    return chosen, weighted


def slot_hits(code, slots):
    ids = lax.broadcasted_iota(jnp.int32, (slots, code.shape[-1]), 0)
    return [code[k : k + 1] == ids for k in range(code.shape[0])]


def gather_kernel(index_ref, code_ref, rows_ref, out_ref, rows, sent, in_sems, out_sems):
    def incoming(i):
        return pltpu.make_async_copy(rows_ref.at[index_ref[i]], rows.at[i], in_sems.at[i])

    def outgoing(i):
        return pltpu.make_async_copy(sent.at[i], out_ref.at[:, i], out_sems.at[i])

    for i in range(NZ):
        incoming(i).start()
    for i in range(NZ):
        hits = slot_hits(code_ref[index_ref[i]], SLICE * CAP)
        pick = sum(jnp.where(hit, 1.0, 0.0) for hit in hits).astype(BF)
        incoming(i).wait()
        chosen = jnp.dot(pick, rows[i], preferred_element_type=F32).astype(BF)
        sent[i] = chosen.reshape(SLICE, CAP, chosen.shape[-1])
        outgoing(i).start()
    for i in range(NZ):
        outgoing(i).wait()


def gather(index, code, all_rows):
    tok, width = all_rows.shape[1:]
    return pl.pallas_call(
        gather_kernel,
        in_specs=[
            pl.BlockSpec(memory_space=pltpu.SMEM),
            pl.BlockSpec(memory_space=pltpu.VMEM),
            pl.BlockSpec(memory_space=pl.ANY),
        ],
        out_specs=pl.BlockSpec(memory_space=pl.ANY),
        scratch_shapes=[
            pltpu.VMEM((NZ, tok, width), BF),
            pltpu.VMEM((NZ, SLICE, CAP, width), BF),
            pltpu.SemaphoreType.DMA((NZ,)),
            pltpu.SemaphoreType.DMA((NZ,)),
        ],
        out_shape=jax.ShapeDtypeStruct((SLICE, NZ, CAP, width), BF),
        compiler_params=pltpu.CompilerParams(vmem_limit_bytes=56 * 1024 * 1024),
        cost_estimate=pl.CostEstimate(
            flops=2 * NZ * SLICE * CAP * tok * width,
            bytes_accessed=4 * NZ * tok * width,
            transcendentals=0,
        ),
        name="gather_rows",
    )(index, code, all_rows)


def combine_kernel(index_ref, code_ref, comb_ref, rows_ref, *refs):
    *carried, out_ref = refs
    comb = comb_ref[0]
    hits = slot_hits(code_ref[0], SLICE * CAP)
    weights = sum(jnp.where(hit, comb[k : k + 1], 0.0) for k, hit in enumerate(hits))
    rows = rows_ref[:, 0].reshape(SLICE * CAP, rows_ref.shape[-1])
    dims = (((0,), (0,)), ((), ()))
    total = lax.dot_general(weights.astype(BF), rows, dims, preferred_element_type=F32)
    out_ref[0] = total.astype(BF)
    for step, carry_ref in enumerate(carried):

        @pl.when(pl.program_id(0) == step)
        def _():
            out_ref[0] = (total + carry_ref[...].astype(F32)).astype(BF)


def combine_rows(index, code, comb, rows, first, count, *carried):
    topk, tok = code.shape[1:]
    width = rows.shape[3]
    tokens = pl.BlockSpec((1, topk, tok), lambda i, index: (index[i], 0, 0))
    return pl.pallas_call(
        combine_kernel,
        grid_spec=pltpu.PrefetchScalarGridSpec(
            num_scalar_prefetch=1,
            grid=(count,),
            in_specs=[
                tokens,
                tokens,
                pl.BlockSpec((SLICE, 1, CAP, width), lambda i, index: (0, i + first, 0, 0)),
            ]
            + [pl.BlockSpec((tok, width), lambda i, index: (0, 0)) for _ in carried],
            out_specs=pl.BlockSpec((1, tok, width), lambda i, index: (i, 0, 0)),
        ),
        out_shape=jax.ShapeDtypeStruct((count, tok, width), BF),
        compiler_params=pltpu.CompilerParams(vmem_limit_bytes=32 * 1024 * 1024),
        cost_estimate=pl.CostEstimate(
            flops=2 * count * SLICE * CAP * tok * width,
            bytes_accessed=4 * count * tok * width,
            transcendentals=0,
        ),
        name="combine_rows",
    )(index, code, comb, rows, *carried)


def around(value, axis, size):
    turned = [value] + [
        lax.ppermute(value, axis, [(i, (i - shift) % size) for i in range(size)])
        for shift in range(1, size)
    ]
    return jnp.roll(jnp.stack(turned), lax.axis_index(axis), axis=0)


def earlier(count):
    size = count.shape[-1]
    rows = lax.broadcasted_iota(jnp.int32, (size, size), 0)
    cols = lax.broadcasted_iota(jnp.int32, (size, size), 1)
    mask = (rows < cols).astype(BF)
    before = lax.dot_general(
        count.astype(BF), mask, (((count.ndim - 1,), (0,)), ((), ())), preferred_element_type=F32
    )
    return before.astype(jnp.int32)


def forward(gate, up):
    sig = jax.nn.sigmoid(gate)
    act = gate * sig
    slope = up * sig * (1.0 + gate * (1.0 - sig))
    return lax.reduce_precision(act * up, 8, 7), act, slope


def backward(saved, dhid):
    hidden, act, slope = saved
    dcomb = lax.reduce_precision(jnp.sum(hidden * dhid, axis=-1), 8, 7)
    return (dhid * slope).astype(BF), (dhid * act).astype(BF), dcomb


def hot_experts(rows_in, rows_cot, mine, other, side):
    both = jnp.concatenate([rows_in, rows_cot], axis=1)
    half = both.shape[2] // 2
    low, high = both[:, :, :half], both[:, :, half:]
    batch = ((0,), (0,))

    def through(rows, weights, dims):
        return lax.dot_general(rows, weights, (dims, batch), preferred_element_type=F32)

    hidden = through(jnp.where(side == 0, low, high), mine, ((2,), (1,)))
    hidden = hidden + through(jnp.where(side == 0, high, low), other, ((2,), (1,)))
    ff = hidden.shape[2] // 3
    count = rows_in.shape[1]
    saved = forward(hidden[:, :count, :ff], hidden[:, :count, ff : 2 * ff])
    dgate, dup, dcomb = backward(saved, hidden[:, count:, 2 * ff :])
    grads = jnp.concatenate([dgate, dup, jnp.zeros_like(dup)], axis=2)
    dx_mine = through(grads, mine, ((2,), (2,))).astype(BF)
    dx_other = through(grads, other, ((2,), (2,))).astype(BF)
    low = jnp.where(side == 0, dx_mine, dx_other)
    high = jnp.where(side == 0, dx_other, dx_mine)
    return jnp.concatenate([low, high], axis=2), dcomb


def shards(inputs, cotangent, routes, router, w_gate, w_up, w_down):
    tok, width = inputs.shape
    topk = routes.shape[1]
    zi, ci, xi = lax.axis_index("z"), lax.axis_index("c"), lax.axis_index("x")
    rows = SLICE * NZ * CAP

    routes_t = routes.T
    in_all = lax.all_gather(inputs, "z")

    part = width // (NC * NZ * NY * NX)

    def quarter(weights):
        blocks = weights.reshape(NC, NZ, NY, NX, part, weights.shape[1])
        return lax.dynamic_index_in_dim(blocks, xi, axis=3, keepdims=False)

    packed = jnp.concatenate([quarter(w_gate[0]), quarter(w_up[0]), quarter(w_down[0].T)], axis=-1)
    cols = packed.shape[-1]
    pieces = exchange(packed.transpose(2, 0, 1, 3, 4).reshape(SLICE, NZ, part, cols), PLANE)

    member = routes_t[:, None, :] == lax.broadcasted_iota(jnp.int32, (1, EXPERTS, 1), 1)
    member_f = member.astype(F32)
    count = jnp.sum(member.astype(jnp.int32), axis=0)
    before = earlier(count)
    is_hot = (jnp.sum(count, axis=1) > CAP).astype(jnp.int32)
    ids = jnp.arange(EXPERTS, dtype=jnp.int32)
    hot_rank = jnp.sum(jnp.where(ids[None, :] < ids[:, None], is_hot[None, :], 0), axis=1)
    hot_pick = is_hot[None, :] * (hot_rank[None, :] == jnp.arange(HOT)[:, None]).astype(jnp.int32)
    hot_id = jnp.sum(hot_pick * ids[None, :], axis=1)
    ks = jnp.arange(topk)
    same = (routes_t[:, None, :] == routes_t[None, :, :]) & (ks[None, :] < ks[:, None])[:, :, None]
    rank = jnp.sum(jnp.where(member, before[None], 0), axis=1) + jnp.sum(same.astype(jnp.int32), axis=1)
    hot_slot = jnp.sum(jnp.where(routes_t[None] == hot_id[:, None, None], 1 + jnp.arange(HOT)[:, None, None], 0), axis=0)
    code = jnp.where(hot_slot > 0, -1, routes_t * CAP + rank)
    hot_code = jnp.where(hot_slot > 0, (hot_slot - 1) * HOT_CAP + rank, -1)
    logits = dot(router, inputs, ((0,), (1,)))
    chosen = jnp.sum(logits[None] * member_f, axis=1)
    expo = jnp.exp(chosen - jnp.max(chosen, axis=0, keepdims=True))
    combine = expo / jnp.sum(expo, axis=0, keepdims=True)
    comb_sent = combine.astype(BF).astype(F32)

    ring = spread_out(jnp.concatenate([code.astype(F32), comb_sent], axis=0), "z", NZ)
    local = ring[:, :topk].astype(jnp.int32) - zi * SLICE * CAP
    comb_all = ring[:, topk:]
    index = (zi + jnp.array(ORDER, jnp.int32)) % NZ
    hot_ids = [hot_id] + [
        lax.ppermute(hot_id, "x", [(i, (i - shift) % NX) for i in range(NX)]) for shift in range(1, NX)
    ]
    sources = zi * SLICE + jnp.arange(SLICE)
    picked = []
    for shift in range(NX):
        wanted = (sources[None, :] == hot_ids[shift][:, None])[:, :, None, None, None]
        picked.append(jnp.sum(jnp.where(wanted, pieces[None], jnp.zeros((), BF)), axis=1, dtype=BF))
    in_all, local, picked, later_cot = lax.optimization_barrier((in_all, local, picked, cotangent))
    cot_all = lax.all_gather(later_cot, "z")
    got = [picked[0]] + [
        lax.ppermute(picked[shift], "x", [(i, (i + shift) % NX) for i in range(NX)])
        for shift in range(1, NX)
    ]
    quarters = jnp.roll(jnp.stack([got[-j % NX] for j in range(NX)]), xi, axis=0)
    held = quarters.transpose(2, 1, 0, 3, 4).reshape(NZ, HOT * NX * part, cols)
    rows_in = exchange(gather(index, local, in_all), PLANE).reshape(rows, width)
    sent_cot = gather(index, local, cot_all)
    hot_rows, hot_rows_comb = selectors(hot_code[None], comb_sent[None], HOT * HOT_CAP)
    hot_in = dot(hot_rows[0], inputs, ((1,), (0,))).astype(BF).reshape(HOT, HOT_CAP, width)
    hot_cot = dot(hot_rows[0], cotangent, ((1,), (0,))).astype(BF).reshape(HOT, HOT_CAP, width)
    rows_in, sent_cot, held, hot_in, hot_cot = lax.optimization_barrier(
        (rows_in, sent_cot, held, hot_in, hot_cot)
    )
    rows_cot = exchange(sent_cot, PLANE).reshape(rows, width)
    held = lax.psum_scatter(held, "z", scatter_dimension=0).reshape(HOT, NX * part, cols)
    held = around(held, "y", NY).transpose(1, 0, 2, 3).reshape(HOT, NY * NX * part, cols)
    saved = forward(dot(rows_in, w_gate[0], ((1,), (0,))), dot(rows_in, w_up[0], ((1,), (0,))))
    rows_cot, saved, held = lax.optimization_barrier((rows_cot, saved, held))
    dgate, dup, dcomb_rows = backward(saved, dot(rows_cot, w_down[0], ((1,), (1,))))

    def input_grads(part_rows):
        def of(rows_of):
            return rows_of.reshape(SLICE, NZ, CAP, -1)[:, part_rows].reshape(-1, rows_of.shape[1])

        grads = dot(of(dgate), w_gate[0], ((1,), (1,))) + dot(of(dup), w_up[0], ((1,), (1,)))
        return grads.astype(BF).reshape(SLICE, -1, CAP, width)

    dpart_far, dpart_near = input_grads(slice(0, FAR)), input_grads(slice(FAR, NZ))
    dcomb_rows = dcomb_rows.reshape(SLICE, NZ, CAP).transpose(1, 0, 2).reshape(NZ, SLICE * CAP)
    placed = (index[None, :] == jnp.arange(NZ)[:, None]).astype(BF)
    dcomb_rows = dot(placed, dcomb_rows.astype(BF), ((1,), (0,))).reshape(EXPERTS, CAP)
    dcomb_rows = jnp.pad(dcomb_rows, ((0, 0), (0, 128 - CAP))).reshape(EXPERTS, 1, 128)
    dcomb_slots = exchange(dcomb_rows, GROUP)
    dpart_far, dpart_near, dcomb_slots = lax.optimization_barrier((dpart_far, dpart_near, dcomb_slots))

    def up_ring(value):
        return lax.ppermute(value, "z", [(i, (i + 1) % NZ) for i in range(NZ)])

    def down_ring(value):
        return lax.ppermute(value, "z", [(i, (i - 1) % NZ) for i in range(NZ)])

    def added(first, second):
        return (first.astype(F32) + second.astype(F32)).astype(BF)

    back_far = exchange(dpart_far, PLANE)
    mine = lax.all_gather(held, "z", axis=1, tiled=True)
    back_far, dpart_near, mine = lax.optimization_barrier((back_far, dpart_near, mine))
    back_near = exchange(dpart_near, PLANE)
    far = combine_rows(index[:FAR], local, comb_all, back_far, 0, FAR)
    rising = up_ring(added(up_ring(far[0]), far[1]))
    falling = down_ring(far[2])

    other = lax.ppermute(mine, "c", [(0, 1), (1, 0)])
    hot_dx, hot_dcomb = hot_experts(hot_in, hot_cot, mine, other, ci)
    hot_grad = dot(hot_rows_comb[0], hot_dx.reshape(HOT * HOT_CAP, width), ((0,), (0,)))

    hot_pick_f = hot_pick.astype(F32)
    cold = 1.0 - jnp.sum(hot_pick_f, axis=0)
    dcomb_slots = dcomb_slots[:, 0, :HOT_CAP] * cold[:, None]
    dcomb_slots = dcomb_slots + jnp.sum(
        hot_pick_f[:, :, None] * hot_dcomb[:, None, :], axis=0
    )
    by_rank = lax.dot_general(
        member.astype(BF), dcomb_slots.astype(BF), (((1,), (0,)), ((), ())), preferred_element_type=F32
    )
    ranked = rank[:, None, :] == lax.broadcasted_iota(jnp.int32, (1, HOT_CAP, 1), 1)
    dcomb = jnp.sum(jnp.where(ranked, by_rank.transpose(0, 2, 1), 0.0), axis=1)
    dlogit = combine * (dcomb - jnp.sum(combine * dcomb, axis=0, keepdims=True))
    spread = jnp.sum(dlogit[:, None, :] * member_f, axis=0).astype(BF)
    local_router = dot(spread, inputs, ((1,), (0,))).reshape(NX, EXPERTS // NX, width)
    local_router = jnp.roll(local_router, -xi, axis=0)
    local_router = local_router[0] + sum(
        lax.ppermute(local_router[shift], "x", [(i, (i + shift) % NX) for i in range(NX)])
        for shift in range(1, NX)
    )
    back_near, rising, falling, far, local_router, hot_grad, spread = lax.optimization_barrier(
        (back_near, rising, falling, far, local_router, hot_grad, spread)
    )
    near_ids = index[FAR:]
    rising = up_ring(added(rising, far[3]))
    falling = down_ring(combine_rows(near_ids[:1], local, comb_all, back_near, 0, 1, falling)[0])
    third = combine_rows(near_ids[1:3], local, comb_all, back_near, 1, 2, rising, falling)
    rising, falling = up_ring(third[0]), down_ring(third[1])
    own = combine_rows(near_ids[3:], local, comb_all, back_near, 3, 1)[0]

    lanes = local_router.size // (SLICE * CAP)
    shares = exchange(local_router.reshape(SLICE, CAP, lanes), PLANE)
    shares = spread_out(jnp.sum(shares, axis=0), "z", NZ)
    shares = spread_out(jnp.sum(shares, axis=0), PLANE, SLICE).reshape(EXPERTS // NX, width)
    grad_router = around(shares, "x", NX).reshape(EXPERTS, width).T

    back = dot(spread, router, ((0,), (1,)))
    grad_inputs = (own.astype(F32) + rising.astype(F32) + falling.astype(F32) + hot_grad + back).astype(BF)
    return grad_inputs, grad_router


def solution(mesh):
    fine = Mesh(mesh.devices.reshape(NZ, NY, NC, NX), ROWS)
    tokens = P(ROWS, None)
    experts = P(GROUP, None, None)
    return jax.shard_map(
        shards,
        mesh=fine,
        in_specs=(tokens, tokens, tokens, P(), experts, experts, experts),
        out_specs=(tokens, P()),
        check_vma=False,
    )
```

```python
import jax
import jax.numpy as jnp
from jax import lax
from jax.experimental import pallas as pl
from jax.experimental.pallas import tpu as pltpu
from jax.sharding import Mesh, PartitionSpec as P

NZ, NY, NC, NX = 8, 4, 2, 4
SLICE = NY * NC
EXPERTS = NZ * SLICE
CAP = 16
HOT = 2
HOT_CAP = 64
ORDER = (4, 3, 5, 2, 6, 1, 7, 0)
FAR = 4
BF = jnp.bfloat16
F32 = jnp.float32
ROWS = ("z", "y", "c", "x")
GROUP = ("z", "y", "c")
PLANE = ("y", "c")


def exchange(value, axes):
    return lax.all_to_all(value, axes, split_axis=0, concat_axis=0, tiled=True)


def spread_out(value, axes, count):
    return exchange(jnp.broadcast_to(value[None], (count,) + value.shape), axes)


def dot(a, b, dims):
    return lax.dot_general(a, b, (dims, ((), ())), preferred_element_type=F32)


def selectors(code, weight, slots):
    ids = lax.broadcasted_iota(jnp.int32, (1, slots, 1), 1)
    hits = code[:, :, None, :] == ids[:, None]
    chosen = jnp.sum(hits.astype(F32), axis=1).astype(BF)
    weighted = jnp.sum(jnp.where(hits, weight[:, :, None, :], 0.0), axis=1).astype(BF)
    return chosen, weighted


def slot_hits(code, slots):
    ids = lax.broadcasted_iota(jnp.int32, (slots, code.shape[-1]), 0)
    return [code[k : k + 1] == ids for k in range(code.shape[0])]


def gather_kernel(index_ref, code_ref, rows_ref, out_ref, rows, sent, in_sems, out_sems):
    def incoming(i):
        return pltpu.make_async_copy(rows_ref.at[index_ref[i]], rows.at[i], in_sems.at[i])

    def outgoing(i):
        return pltpu.make_async_copy(sent.at[i], out_ref.at[:, i], out_sems.at[i])

    for i in range(NZ):
        incoming(i).start()
    for i in range(NZ):
        hits = slot_hits(code_ref[index_ref[i]], SLICE * CAP)
        pick = sum(jnp.where(hit, 1.0, 0.0) for hit in hits).astype(BF)
        incoming(i).wait()
        chosen = jnp.dot(pick, rows[i], preferred_element_type=F32).astype(BF)
        sent[i] = chosen.reshape(SLICE, CAP, chosen.shape[-1])
        outgoing(i).start()
    for i in range(NZ):
        outgoing(i).wait()


def gather(index, code, all_rows):
    tok, width = all_rows.shape[1:]
    return pl.pallas_call(
        gather_kernel,
        in_specs=[
            pl.BlockSpec(memory_space=pltpu.SMEM),
            pl.BlockSpec(memory_space=pltpu.VMEM),
            pl.BlockSpec(memory_space=pl.ANY),
        ],
        out_specs=pl.BlockSpec(memory_space=pl.ANY),
        scratch_shapes=[
            pltpu.VMEM((NZ, tok, width), BF),
            pltpu.VMEM((NZ, SLICE, CAP, width), BF),
            pltpu.SemaphoreType.DMA((NZ,)),
            pltpu.SemaphoreType.DMA((NZ,)),
        ],
        out_shape=jax.ShapeDtypeStruct((SLICE, NZ, CAP, width), BF),
        compiler_params=pltpu.CompilerParams(vmem_limit_bytes=56 * 1024 * 1024),
        cost_estimate=pl.CostEstimate(
            flops=2 * NZ * SLICE * CAP * tok * width,
            bytes_accessed=4 * NZ * tok * width,
            transcendentals=0,
        ),
        name="gather_rows",
    )(index, code, all_rows)


def combine_kernel(index_ref, code_ref, comb_ref, rows_ref, *refs):
    *carried, out_ref = refs
    comb = comb_ref[0]
    hits = slot_hits(code_ref[0], SLICE * CAP)
    weights = sum(jnp.where(hit, comb[k : k + 1], 0.0) for k, hit in enumerate(hits))
    rows = rows_ref[:, 0].reshape(SLICE * CAP, rows_ref.shape[-1])
    dims = (((0,), (0,)), ((), ()))
    total = lax.dot_general(weights.astype(BF), rows, dims, preferred_element_type=F32)
    out_ref[0] = total.astype(BF)
    for step, carry_ref in enumerate(carried):

        @pl.when(pl.program_id(0) == step)
        def _():
            out_ref[0] = (total + carry_ref[...].astype(F32)).astype(BF)


def combine_rows(index, code, comb, rows, first, count, *carried):
    topk, tok = code.shape[1:]
    width = rows.shape[3]
    tokens = pl.BlockSpec((1, topk, tok), lambda i, index: (index[i], 0, 0))
    return pl.pallas_call(
        combine_kernel,
        grid_spec=pltpu.PrefetchScalarGridSpec(
            num_scalar_prefetch=1,
            grid=(count,),
            in_specs=[
                tokens,
                tokens,
                pl.BlockSpec((SLICE, 1, CAP, width), lambda i, index: (0, i + first, 0, 0)),
            ]
            + [pl.BlockSpec((tok, width), lambda i, index: (0, 0)) for _ in carried],
            out_specs=pl.BlockSpec((1, tok, width), lambda i, index: (i, 0, 0)),
        ),
        out_shape=jax.ShapeDtypeStruct((count, tok, width), BF),
        compiler_params=pltpu.CompilerParams(vmem_limit_bytes=32 * 1024 * 1024),
        cost_estimate=pl.CostEstimate(
            flops=2 * count * SLICE * CAP * tok * width,
            bytes_accessed=4 * count * tok * width,
            transcendentals=0,
        ),
        name="combine_rows",
    )(index, code, comb, rows, *carried)


def around(value, axis, size):
    turned = [value] + [
        lax.ppermute(value, axis, [(i, (i - shift) % size) for i in range(size)])
        for shift in range(1, size)
    ]
    return jnp.roll(jnp.stack(turned), lax.axis_index(axis), axis=0)


def earlier(count):
    size = count.shape[-1]
    rows = lax.broadcasted_iota(jnp.int32, (size, size), 0)
    cols = lax.broadcasted_iota(jnp.int32, (size, size), 1)
    mask = (rows < cols).astype(BF)
    before = lax.dot_general(
        count.astype(BF), mask, (((count.ndim - 1,), (0,)), ((), ())), preferred_element_type=F32
    )
    return before.astype(jnp.int32)


def forward(gate, up):
    sig = jax.nn.sigmoid(gate)
    act = gate * sig
    slope = up * sig * (1.0 + gate * (1.0 - sig))
    return lax.reduce_precision(act * up, 8, 7), act, slope


def backward(saved, dhid):
    hidden, act, slope = saved
    dcomb = lax.reduce_precision(jnp.sum(hidden * dhid, axis=-1), 8, 7)
    return (dhid * slope).astype(BF), (dhid * act).astype(BF), dcomb


def hot_experts(rows_in, rows_cot, mine, other, side):
    both = jnp.concatenate([rows_in, rows_cot], axis=1)
    half = both.shape[2] // 2
    low, high = both[:, :, :half], both[:, :, half:]
    batch = ((0,), (0,))

    def through(rows, weights, dims):
        return lax.dot_general(rows, weights, (dims, batch), preferred_element_type=F32)

    hidden = through(jnp.where(side == 0, low, high), mine, ((2,), (1,)))
    hidden = hidden + through(jnp.where(side == 0, high, low), other, ((2,), (1,)))
    ff = hidden.shape[2] // 3
    count = rows_in.shape[1]
    saved = forward(hidden[:, :count, :ff], hidden[:, :count, ff : 2 * ff])
    dgate, dup, dcomb = backward(saved, hidden[:, count:, 2 * ff :])
    grads = jnp.concatenate([dgate, dup, jnp.zeros_like(dup)], axis=2)
    dx_mine = through(grads, mine, ((2,), (2,))).astype(BF)
    dx_other = through(grads, other, ((2,), (2,))).astype(BF)
    low = jnp.where(side == 0, dx_mine, dx_other)
    high = jnp.where(side == 0, dx_other, dx_mine)
    return jnp.concatenate([low, high], axis=2), dcomb


def shards(inputs, cotangent, routes, router, w_gate, w_up, w_down):
    tok, width = inputs.shape
    topk = routes.shape[1]
    zi, ci, xi = lax.axis_index("z"), lax.axis_index("c"), lax.axis_index("x")
    rows = SLICE * NZ * CAP

    routes_t = routes.T
    in_all = lax.all_gather(inputs, "z")

    part = width // (NC * NZ * NY * NX)

    def quarter(weights):
        blocks = weights.reshape(NC, NZ, NY, NX, part, weights.shape[1])
        return lax.dynamic_index_in_dim(blocks, xi, axis=3, keepdims=False)

    packed = jnp.concatenate([quarter(w_gate[0]), quarter(w_up[0]), quarter(w_down[0].T)], axis=-1)
    cols = packed.shape[-1]
    pieces = exchange(packed.transpose(2, 0, 1, 3, 4).reshape(SLICE, NZ, part, cols), PLANE)

    member = routes_t[:, None, :] == lax.broadcasted_iota(jnp.int32, (1, EXPERTS, 1), 1)
    member_f = member.astype(F32)
    count = jnp.sum(member.astype(jnp.int32), axis=0)
    before = earlier(count)
    is_hot = (jnp.sum(count, axis=1) > CAP).astype(jnp.int32)
    ids = jnp.arange(EXPERTS, dtype=jnp.int32)
    hot_rank = jnp.sum(jnp.where(ids[None, :] < ids[:, None], is_hot[None, :], 0), axis=1)
    hot_pick = is_hot[None, :] * (hot_rank[None, :] == jnp.arange(HOT)[:, None]).astype(jnp.int32)
    hot_id = jnp.sum(hot_pick * ids[None, :], axis=1)
    ks = jnp.arange(topk)
    same = (routes_t[:, None, :] == routes_t[None, :, :]) & (ks[None, :] < ks[:, None])[:, :, None]
    rank = jnp.sum(jnp.where(member, before[None], 0), axis=1) + jnp.sum(same.astype(jnp.int32), axis=1)
    hot_slot = jnp.sum(jnp.where(routes_t[None] == hot_id[:, None, None], 1 + jnp.arange(HOT)[:, None, None], 0), axis=0)
    code = jnp.where(hot_slot > 0, -1, routes_t * CAP + rank)
    hot_code = jnp.where(hot_slot > 0, (hot_slot - 1) * HOT_CAP + rank, -1)
    logits = dot(router, inputs, ((0,), (1,)))
    chosen = jnp.sum(logits[None] * member_f, axis=1)
    expo = jnp.exp(chosen - jnp.max(chosen, axis=0, keepdims=True))
    combine = expo / jnp.sum(expo, axis=0, keepdims=True)
    comb_sent = combine.astype(BF).astype(F32)

    ring = spread_out(jnp.concatenate([code.astype(F32), comb_sent], axis=0), "z", NZ)
    local = ring[:, :topk].astype(jnp.int32) - zi * SLICE * CAP
    comb_all = ring[:, topk:]
    index = (zi + jnp.array(ORDER, jnp.int32)) % NZ
    hot_ids = [hot_id] + [
        lax.ppermute(hot_id, "x", [(i, (i - shift) % NX) for i in range(NX)]) for shift in range(1, NX)
    ]
    sources = zi * SLICE + jnp.arange(SLICE)
    picked = []
    for shift in range(NX):
        wanted = (sources[None, :] == hot_ids[shift][:, None])[:, :, None, None, None]
        picked.append(jnp.sum(jnp.where(wanted, pieces[None], jnp.zeros((), BF)), axis=1, dtype=BF))
    in_all, local, picked, later_cot = lax.optimization_barrier((in_all, local, picked, cotangent))
    cot_all = lax.all_gather(later_cot, "z")
    got = [picked[0]] + [
        lax.ppermute(picked[shift], "x", [(i, (i + shift) % NX) for i in range(NX)])
        for shift in range(1, NX)
    ]
    quarters = jnp.roll(jnp.stack([got[-j % NX] for j in range(NX)]), xi, axis=0)
    held = quarters.transpose(2, 1, 0, 3, 4).reshape(NZ, HOT * NX * part, cols)
    rows_in = exchange(gather(index, local, in_all), PLANE).reshape(rows, width)
    sent_cot = gather(index, local, cot_all)
    hot_rows, hot_rows_comb = selectors(hot_code[None], comb_sent[None], HOT * HOT_CAP)
    hot_in = dot(hot_rows[0], inputs, ((1,), (0,))).astype(BF).reshape(HOT, HOT_CAP, width)
    hot_cot = dot(hot_rows[0], cotangent, ((1,), (0,))).astype(BF).reshape(HOT, HOT_CAP, width)
    rows_in, sent_cot, held, hot_in, hot_cot = lax.optimization_barrier(
        (rows_in, sent_cot, held, hot_in, hot_cot)
    )
    rows_cot = exchange(sent_cot, PLANE).reshape(rows, width)
    held = lax.psum_scatter(held, "z", scatter_dimension=0).reshape(HOT, NX * part, cols)
    held = around(held, "y", NY).transpose(1, 0, 2, 3).reshape(HOT, NY * NX * part, cols)
    saved = forward(dot(rows_in, w_gate[0], ((1,), (0,))), dot(rows_in, w_up[0], ((1,), (0,))))
    rows_cot, saved, held = lax.optimization_barrier((rows_cot, saved, held))
    dgate, dup, dcomb_rows = backward(saved, dot(rows_cot, w_down[0], ((1,), (1,))))

    def input_grads(part_rows):
        def of(rows_of):
            return rows_of.reshape(SLICE, NZ, CAP, -1)[:, part_rows].reshape(-1, rows_of.shape[1])

        grads = dot(of(dgate), w_gate[0], ((1,), (1,))) + dot(of(dup), w_up[0], ((1,), (1,)))
        return grads.astype(BF).reshape(SLICE, -1, CAP, width)

    dpart_far, dpart_near = input_grads(slice(0, FAR)), input_grads(slice(FAR, NZ))
    dcomb_rows = dcomb_rows.reshape(SLICE, NZ, CAP).transpose(1, 0, 2).reshape(NZ, SLICE * CAP)
    placed = (index[None, :] == jnp.arange(NZ)[:, None]).astype(BF)
    dcomb_rows = dot(placed, dcomb_rows.astype(BF), ((1,), (0,))).reshape(EXPERTS, CAP)
    dcomb_rows = jnp.pad(dcomb_rows, ((0, 0), (0, 128 - CAP))).reshape(EXPERTS, 1, 128)
    dcomb_slots = exchange(dcomb_rows, GROUP)
    dpart_far, dpart_near, dcomb_slots = lax.optimization_barrier((dpart_far, dpart_near, dcomb_slots))

    def up_ring(value):
        return lax.ppermute(value, "z", [(i, (i + 1) % NZ) for i in range(NZ)])

    def down_ring(value):
        return lax.ppermute(value, "z", [(i, (i - 1) % NZ) for i in range(NZ)])

    def added(first, second):
        return (first.astype(F32) + second.astype(F32)).astype(BF)

    back_far = exchange(dpart_far, PLANE)
    mine = lax.all_gather(held, "z", axis=1, tiled=True)
    back_far, dpart_near, mine = lax.optimization_barrier((back_far, dpart_near, mine))
    back_near = exchange(dpart_near, PLANE)
    far = combine_rows(index[:FAR], local, comb_all, back_far, 0, FAR)
    rising = up_ring(added(up_ring(far[0]), far[1]))
    falling = down_ring(far[2])

    other = lax.ppermute(mine, "c", [(0, 1), (1, 0)])
    hot_dx, hot_dcomb = hot_experts(hot_in, hot_cot, mine, other, ci)
    hot_grad = dot(hot_rows_comb[0], hot_dx.reshape(HOT * HOT_CAP, width), ((0,), (0,)))

    hot_pick_f = hot_pick.astype(F32)
    cold = 1.0 - jnp.sum(hot_pick_f, axis=0)
    dcomb_slots = dcomb_slots[:, 0, :HOT_CAP] * cold[:, None]
    dcomb_slots = dcomb_slots + jnp.sum(
        hot_pick_f[:, :, None] * hot_dcomb[:, None, :], axis=0
    )
    by_rank = lax.dot_general(
        member.astype(BF), dcomb_slots.astype(BF), (((1,), (0,)), ((), ())), preferred_element_type=F32
    )
    ranked = rank[:, None, :] == lax.broadcasted_iota(jnp.int32, (1, HOT_CAP, 1), 1)
    dcomb = jnp.sum(jnp.where(ranked, by_rank.transpose(0, 2, 1), 0.0), axis=1)
    dlogit = combine * (dcomb - jnp.sum(combine * dcomb, axis=0, keepdims=True))
    spread = jnp.sum(dlogit[:, None, :] * member_f, axis=0).astype(BF)
    local_router = dot(spread, inputs, ((1,), (0,))).reshape(NX, EXPERTS // NX, width)
    local_router = jnp.roll(local_router, -xi, axis=0)
    local_router = local_router[0] + sum(
        lax.ppermute(local_router[shift], "x", [(i, (i + shift) % NX) for i in range(NX)])
        for shift in range(1, NX)
    )
    back_near, rising, falling, far, local_router, hot_grad, spread = lax.optimization_barrier(
        (back_near, rising, falling, far, local_router, hot_grad, spread)
    )
    near_ids = index[FAR:]
    rising = up_ring(added(rising, far[3]))
    lanes = local_router.size // (SLICE * CAP)
    shares = exchange(local_router.reshape(SLICE, CAP, lanes), PLANE)
    shares, back_near = lax.optimization_barrier((shares, back_near))
    shares = spread_out(jnp.sum(shares, axis=0), "z", NZ)
    falling = down_ring(combine_rows(near_ids[:1], local, comb_all, back_near, 0, 1, falling)[0])
    shares, rising, falling = lax.optimization_barrier((shares, rising, falling))
    third = combine_rows(near_ids[1:3], local, comb_all, back_near, 1, 2, rising, falling)
    rising, falling = up_ring(third[0]), down_ring(third[1])
    own = combine_rows(near_ids[3:], local, comb_all, back_near, 3, 1)[0]
    shares = spread_out(jnp.sum(shares, axis=0), PLANE, SLICE).reshape(EXPERTS // NX, width)
    grad_router = around(shares, "x", NX).reshape(EXPERTS, width).T

    back = dot(spread, router, ((0,), (1,)))
    grad_inputs = (own.astype(F32) + rising.astype(F32) + falling.astype(F32) + hot_grad + back).astype(BF)
    return grad_inputs, grad_router


def solution(mesh):
    fine = Mesh(mesh.devices.reshape(NZ, NY, NC, NX), ROWS)
    tokens = P(ROWS, None)
    experts = P(GROUP, None, None)
    return jax.shard_map(
        shards,
        mesh=fine,
        in_specs=(tokens, tokens, tokens, P(), experts, experts, experts),
        out_specs=(tokens, P()),
        check_vma=False,
    )
```
